32 devices in a mesh: lib: 2 (over x), hit: 8 (over z, y), lm: 2 (over core).
Axes of the slice: x: 2, y: 2, z: 4, core: 2. Of those that a mesh axis runs over, the one named last changes fastest.
Arguments:
- fingerprints: int32 [8192, 128], P(('lib', 'hit')), parts along dimension 0, may hold values from 0 to 65535, as said below
- pick_list: int32 [8192], P(('lib', 'lm')), parts along dimension 0, may hold values from 0 to 4095, as said below
- inverse_root: bfloat16 [8192, 2, 2048], P('lib', 'lm', 'hit'), parts along dimension 0, may hold values from -0.09375 to 0.09375
Outputs:
- embedding: bfloat16 [8192, 4096], P(('lib', 'hit'), 'lm'), parts along dimension 0
The draws below stay inside these ranges and needn't reach their ends.
There are 2 independent parts, one for each index of `lib`. The reference program is written for one: setup_inputs(seed, part) draws one part's arguments, and reference() takes and returns one part's arrays. A program takes and returns all parts, laid end to end along the dimension named above; each array names one. Nothing has to cross between parts.
Inputs may be any that keep to these rules, and one draw needn't show every extreme that they name: `pick_list`: within each half of the list, at most 768 picks lie in any one aligned block of 512 hits, and exactly 768 lie in one such block. `fingerprints`: every fingerprint has the lowest bit of its first word set.
All inputs are finite; a program needn't handle non-finite values.
Results may differ from the reference program's by a relative error of at most 0.0049.
Values may be sent and summed in bfloat16 or wider, within the bound.
No kernel may reach another device: no remote copies, remote signals or barrier semaphores. Data moves between devices by JAX's collectives and lax.ppermute only.
A program may use at most 128 MiB of HBM per device.

```python
import jax
import jax.numpy as jnp

LM = 4096
H_DEV = 512
WORDS = 128
HITS = 4096
CAP = 768
N_HIT = 8


def draw_fingerprints(key, part):
    key = jax.random.fold_in(key, 11)
    keys = jax.random.split(key, 4)
    powers = jnp.left_shift(jnp.int32(1), jnp.arange(16, dtype=jnp.int32))
    scaffold = (jax.random.randint(keys[0], (64, WORDS, 16), 0, 100) < 15).astype(jnp.int32)
    family = jax.random.randint(keys[1], (HITS,), 0, 64)
    percent = jax.random.randint(keys[2], (HITS, 1, 1), 3, 40)
    own_bits = (jax.random.randint(keys[3], (HITS, WORDS, 16), 0, 100) < percent).astype(jnp.int32)
    flags = jnp.maximum(scaffold[family], own_bits)
    flags = flags.at[0, WORDS - 1, :].set(1)
    flags = flags.at[1, WORDS - 1, :].set(0)
    flags = flags.at[:, 0, 0].set(1)
    return jnp.sum(flags * powers[None, None, :], axis=2).astype(jnp.int32)


def block_totals(key):
    keys = jax.random.split(key, 3)
    heavy = jax.random.randint(keys[0], (), 0, N_HIT)
    leftover = LM // 2 - CAP
    base_count = leftover // (N_HIT - 1)
    surplus = leftover - base_count * (N_HIT - 1)
    others = jnp.arange(N_HIT - 1, dtype=jnp.int32)
    counts = base_count + (others < surplus).astype(jnp.int32)
    pair_count = (N_HIT - 1) // 2
    moved = jax.random.randint(keys[1], (pair_count,), 0, base_count // 2 + 1)
    counts = counts.at[0:2 * pair_count:2].add(moved).at[1:2 * pair_count:2].add(-moved)
    counts = counts[jax.random.permutation(keys[2], N_HIT - 1)]
    other_owner = others + (others >= heavy).astype(jnp.int32)
    return jnp.zeros((N_HIT,), jnp.int32).at[other_owner].set(counts).at[heavy].set(CAP)


def place_half(key, totals, start_at, stride, offsets):
    ends = jnp.cumsum(totals)
    begins = ends - totals
    places = jnp.arange(LM // 2, dtype=jnp.int32)
    holder = jnp.sum((places[:, None] >= ends[None, :]).astype(jnp.int32), axis=1)
    position = places - begins[holder] + start_at[holder]
    row_local = (position * stride + offsets[holder]) % H_DEV
    chosen = holder * H_DEV + row_local
    return chosen[jax.random.permutation(key, LM // 2)].astype(jnp.int32)


def draw_pick_list(key, part):
    key = jax.random.fold_in(key, 23)
    shared = jax.random.split(jax.random.fold_in(key, 3), 2)
    stride = 2 * jax.random.randint(shared[0], (), 0, max(H_DEV // 2, 1)) + 1
    offsets = jax.random.randint(shared[1], (N_HIT,), 0, H_DEV)
    offsets = offsets.at[0].set(0).at[N_HIT - 1].set(H_DEV - 1)
    first_totals = block_totals(jax.random.fold_in(key, 1))
    second_totals = block_totals(jax.random.fold_in(key, 2))
    no_start = jnp.zeros((N_HIT,), jnp.int32)
    first = place_half(jax.random.fold_in(key, 11), first_totals, no_start, stride, offsets)
    second = place_half(jax.random.fold_in(key, 12), second_totals, first_totals, stride, offsets)
    return jnp.concatenate([first, second]).astype(jnp.int32)


def block_levels(stream_key, extent, cuts, low, high):
    loudness = 1.0
    for axis_at, blocks in cuts:
        draws = jax.random.uniform(jax.random.fold_in(jax.random.fold_in(stream_key, 6), axis_at), (blocks,), jnp.float32, low / len(cuts), high / len(cuts))
        loudness = loudness * jnp.repeat(jnp.exp(draws), extent[axis_at] // blocks).reshape((-1,) + (1,) * (len(extent) - 1 - axis_at))
    return loudness


def centred(own_key, extent, spread, most, pieces=(), held_as=jnp.bfloat16):
    values = jax.random.normal(own_key, extent, jnp.float32) * spread
    if len(pieces) > 0:
        values = block_levels(own_key, extent, pieces, -0.22, 0.18) * values
    return jnp.clip(values, min=-most, max=most).astype(held_as)


def setup_inputs(seed: int = 0, part: int = 0) -> dict:
    splits = jax.random.split(jax.random.key(seed), 4)
    part_keys = jax.random.split(jax.random.fold_in(splits[3], part), 4)
    fingerprints = draw_fingerprints(jax.random.fold_in(jax.random.fold_in(splits[3], part), 71), part)
    pick_list = draw_pick_list(jax.random.fold_in(jax.random.fold_in(splits[3], part), 71), part)
    inverse_root = centred(part_keys[2], (LM, 2, LM // 2), LM ** -0.5, 0.09375, ((1, 2), (2, 8)))
    return dict(fingerprints=fingerprints, pick_list=pick_list, inverse_root=inverse_root)


def unpack_words(packed):
    shifts = jnp.arange(16, dtype=jnp.int32)
    flags = jnp.bitwise_and(jnp.right_shift(packed[:, :, None], shifts[None, None, :]), 1)
    return flags.reshape(packed.shape[0], packed.shape[1] * 16).astype(jnp.bfloat16)


def reference(fingerprints, pick_list, inverse_root):
    hit_bits = unpack_words(fingerprints)
    landmark_bits = hit_bits[pick_list.astype(jnp.int32)]
    common = jnp.dot(hit_bits, landmark_bits.T, preferred_element_type=jnp.float32)
    hit_count = jnp.sum(hit_bits.astype(jnp.float32), axis=1)
    landmark_count = jnp.sum(landmark_bits.astype(jnp.float32), axis=1)
    kernel = (common / (hit_count[:, None] + landmark_count[None, :] - common)).astype(jnp.bfloat16)
    matrix = inverse_root.reshape(LM, LM)
    return jnp.dot(kernel, matrix, preferred_element_type=jnp.float32).astype(jnp.bfloat16)
```

```python
import functools

import jax
import jax.numpy as jnp
from jax import lax
from jax.experimental import pallas as pl
from jax.experimental.pallas import tpu as pltpu
from jax.sharding import PartitionSpec as P

F8 = jnp.float8_e4m3fn
BITS = 16
VMEM = pl.BlockSpec(memory_space=pltpu.VMEM)
SMEM = pl.BlockSpec(memory_space=pltpu.SMEM)


def unpack_kernel(*refs):
    half = len(refs) // 3
    for word_ref, bits_ref, count_ref in zip(refs[:half], refs[half::2], refs[half + 1 :: 2]):
        words = word_ref[...].astype(jnp.int32)
        count = jnp.sum(lax.population_count(words).astype(jnp.float32), axis=1, keepdims=True)
        count_ref[...] = jnp.broadcast_to(count, count_ref.shape)
        width = words.shape[1]
        for bit in range(BITS):
            flag = ((words >> bit) & 1).astype(jnp.int8)
            bits_ref[:, bit * width : (bit + 1) * width] = flag.astype(F8)


def unpack(blocks):
    shapes = []
    for block in blocks:
        rows, width = block.shape
        shapes.append(jax.ShapeDtypeStruct((rows, BITS * width), F8))
        shapes.append(jax.ShapeDtypeStruct((rows, 128), jnp.float32))
    out = pl.pallas_call(
        unpack_kernel,
        in_specs=[VMEM] * len(blocks),
        out_specs=[VMEM] * len(shapes),
        out_shape=shapes,
        compiler_params=pltpu.CompilerParams(vmem_limit_bytes=24 * 2**20),
        name="unpack",
    )(*blocks)
    return [(out[2 * i], out[2 * i + 1]) for i in range(len(blocks))]


def spread_kernel(base_ref, pick_ref, weight_ref, out_ref, *, sub, chunk):
    step = pl.program_id(0)
    tile = out_ref.shape[1]
    parts = [
        lax.broadcasted_iota(jnp.int32, (sub, 1), 0) + base_ref[step * (tile // sub) + i]
        for i in range(tile // sub)
    ]
    ids = jnp.concatenate(parts, axis=0)
    total = None
    for start in range(0, weight_ref.shape[0], chunk):
        hot = jnp.where(pick_ref[0:1, start : start + chunk] == ids, 1.0, 0.0).astype(jnp.bfloat16)
        part = jnp.dot(
            hot, weight_ref[start : start + chunk, :], preferred_element_type=jnp.float32
        )
        total = part if total is None else total + part
    out_ref[...] = total.T.astype(jnp.bfloat16)


def spread(base, picks, weight, sub, tile=1024, chunk=512):
    marks, cols = weight.shape
    hits = base.shape[0] * sub
    return pl.pallas_call(
        functools.partial(spread_kernel, sub=sub, chunk=chunk),
        grid_spec=pltpu.PrefetchScalarGridSpec(
            num_scalar_prefetch=1,
            grid=(hits // tile,),
            in_specs=[
                pl.BlockSpec((1, marks), lambda i, base: (0, 0)),
                pl.BlockSpec((marks, cols), lambda i, base: (0, 0)),
            ],
            out_specs=pl.BlockSpec((cols, tile), lambda i, base: (0, i)),
        ),
        out_shape=jax.ShapeDtypeStruct((cols, hits), jnp.bfloat16),
        compiler_params=pltpu.CompilerParams(vmem_limit_bytes=24 * 2**20),
        cost_estimate=pl.CostEstimate(
            flops=2 * marks * cols * hits, bytes_accessed=4 * marks * cols, transcendentals=0
        ),
        name="spread",
    )(base, picks, weight)


def block_kernel(words_ref, own_ref, sib_ref, *refs):
    out_ref, flags, kern = refs[-3:]
    pairs = refs[:-3]
    words = words_ref[...].astype(jnp.int32).T
    width = words.shape[0]
    count = jnp.sum(lax.population_count(words).astype(jnp.float32), axis=0, keepdims=True)
    for bit in range(BITS):
        flag = ((words >> bit) & 1).astype(jnp.int8)
        flags[bit * width : (bit + 1) * width, :] = flag.astype(F8)
    at = 0
    for bits_ref, count_ref in zip(pairs[::2], pairs[1::2]):
        rows = bits_ref.shape[0]
        common = jnp.dot(bits_ref[...], flags[...], preferred_element_type=jnp.float32)
        union = (count + count_ref[:, 0:1]) - common
        kern[at : at + rows, :] = (common / union).astype(jnp.bfloat16)
        at += rows
    mid = at // 2
    own = jnp.dot(own_ref[...], kern[...], preferred_element_type=jnp.float32)
    out_ref[0] = own.T.astype(jnp.bfloat16)
    sib = jnp.dot(sib_ref[:, mid:], kern[:mid, :], preferred_element_type=jnp.float32)
    sib += jnp.dot(sib_ref[:, :mid], kern[mid:, :], preferred_element_type=jnp.float32)
    out_ref[1] = sib.T.astype(jnp.bfloat16)


def block(words, own, sib, pairs):
    rows, width = words.shape
    cols = own.shape[0]
    hits = own.shape[1]
    flat = [x for pair in pairs for x in pair]
    return pl.pallas_call(
        block_kernel,
        in_specs=[VMEM] * (3 + len(flat)),
        out_specs=VMEM,
        out_shape=jax.ShapeDtypeStruct((2, rows, cols), jnp.bfloat16),
        scratch_shapes=[
            pltpu.VMEM((BITS * width, rows), F8),
            pltpu.VMEM((hits, rows), jnp.bfloat16),
        ],
        compiler_params=pltpu.CompilerParams(vmem_limit_bytes=32 * 2**20),
        cost_estimate=pl.CostEstimate(
            flops=2 * hits * rows * (BITS * width // 2 + 2 * cols),
            bytes_accessed=rows * cols * 4,
            transcendentals=0,
        ),
        name="block",
    )(words, own, sib, *flat)


def gather_kernel(place_ref, *refs):
    out_ref = refs[-1]
    count = (len(refs) - 1) // 2
    for k in range(count):
        own_ref, sib_ref = refs[2 * k], refs[2 * k + 1]
        rows, cols = sib_ref.shape
        col = pl.ds(pl.multiple_of(place_ref[k + 1] * cols, cols), cols)
        side = place_ref[0]
        out_ref[pl.ds(pl.multiple_of(side * rows, rows), rows), col] = own_ref[0]
        out_ref[pl.ds(pl.multiple_of((1 - side) * rows, rows), rows), col] = sib_ref[...]


def small(fingerprints, pick_list, inverse_root):
    hit_rows, width = fingerprints.shape
    devices = lax.axis_size("hit")
    me = lax.axis_index("hit")
    side = lax.axis_index("lm")
    half = hit_rows // 2
    weight = inverse_root[:, 0, :]
    cols = weight.shape[1]
    swap = [(0, 1), (1, 0)]

    def across(x, k):
        return lax.ppermute(x, "hit", [(i, i ^ k) for i in range(devices)])

    def over(x):
        return lax.ppermute(x, "lm", swap)

    other_picks = over(pick_list)
    packed = fingerprints.astype(jnp.uint16)
    mine = lax.dynamic_slice_in_dim(packed, side * half, half)
    theirs = lax.dynamic_slice_in_dim(packed, (1 - side) * half, half)
    order = list(range(devices - 1, 0, -1))
    own_words = {0: mine}
    for k in order:
        own_words[k] = across(mine, k)
    sib_words = {0: theirs}
    for k in order:
        sib_words[k] = over(own_words[k])

    both = jnp.stack([pick_list, other_picks])
    picks = jnp.where(side == 0, both, both[::-1]).reshape(1, -1)
    slots = jnp.arange(devices)
    tops = (slots ^ me) * hit_rows
    base = jnp.concatenate([tops + side * half, tops + (1 - side) * half]).astype(jnp.int32)
    own_sums = spread(base, picks, weight, half)
    sib_sums = over(own_sums)

    own_pairs = dict()
    sib_pairs = dict()
    own_pairs[0], sib_pairs[0] = unpack([mine, theirs])
    near = [k for k in order if k < devices // 2]
    far = [k for k in order if k >= devices // 2]
    for group, words, pairs in (
        (near, own_words, own_pairs),
        (near, sib_words, sib_pairs),
        (far, own_words, own_pairs),
        (far, sib_words, sib_pairs),
    ):
        pairs.update(zip(group, unpack([words[k] for k in group])))
    pairs = [own_pairs[k] for k in range(devices)] + [sib_pairs[k] for k in range(devices)]

    pieces = []
    for k in order + [0]:
        made = block(own_words[k], own_sums, sib_sums, pairs)
        got = made if k == 0 else across(made, k)
        pieces.append((k, got, over(got[1])))

    place = jnp.stack([side] + [k ^ me for k, _, _ in pieces]).astype(jnp.int32)
    flat = [x for _, got, sib in pieces for x in (got, sib)]
    return pl.pallas_call(
        gather_kernel,
        in_specs=[SMEM] + [VMEM] * len(flat),
        out_specs=VMEM,
        out_shape=jax.ShapeDtypeStruct((hit_rows, devices * cols), jnp.bfloat16),
        compiler_params=pltpu.CompilerParams(vmem_limit_bytes=24 * 2**20),
        name="place",
    )(place, *flat)


def large(fingerprints, pick_list, inverse_root):
    hit_rows, width = fingerprints.shape
    devices = lax.axis_size("hit")
    side = lax.axis_index("lm")
    half = hit_rows // 2
    weight = inverse_root[:, 0, :]
    cols = weight.shape[1]
    picks = lax.all_gather(pick_list, "lm", tiled=True)
    words = lax.all_gather(fingerprints, "hit", tiled=True)
    hits = words.shape[0]
    blocks = words.reshape(devices, hit_rows, width)

    def spread_block(index):
        hot = (index * hit_rows + jnp.arange(hit_rows))[:, None] == picks[None, :]
        made = jnp.dot(hot.astype(jnp.bfloat16), weight, preferred_element_type=jnp.float32)
        return made.astype(jnp.bfloat16)

    def flag_block(block_words):
        flags = [((block_words >> bit) & 1).astype(F8) for bit in range(BITS)]
        return jnp.concatenate(flags, axis=1)

    sums = lax.map(spread_block, jnp.arange(devices)).reshape(hits, cols)
    sums = lax.all_gather(sums, "lm", axis=1, tiled=True)
    bits = lax.map(flag_block, blocks).reshape(hits, BITS * width)
    count = jnp.sum(lax.population_count(words), axis=1).astype(jnp.float32)

    def one(index):
        start = index * hit_rows + side * half
        rows = lax.dynamic_slice_in_dim(bits, start, half)
        common = lax.dot_general(
            rows, bits, (((1,), (1,)), ((), ())), preferred_element_type=jnp.float32
        )
        union = lax.dynamic_slice_in_dim(count, start, half)[:, None] + count[None, :] - common
        kernel = (common / union).astype(jnp.bfloat16)
        return jnp.dot(kernel, sums, preferred_element_type=jnp.float32).astype(jnp.bfloat16)

    made = lax.map(one, jnp.arange(devices))
    got = lax.all_to_all(made, "hit", 0, 0, tiled=True)
    got = got.reshape(devices, half, 2, cols).transpose(2, 1, 0, 3)
    got = got.reshape(2, 1, half, devices * cols)
    return lax.all_to_all(got, "lm", 0, 1, tiled=True).reshape(hit_rows, devices * cols)


def local(fingerprints, pick_list, inverse_root):
    if lax.axis_size("hit") > 8:
        return large(fingerprints, pick_list, inverse_root)
    return small(fingerprints, pick_list, inverse_root)


def solution(mesh):
    placed = (P(("lib", "hit"), None), P(("lib", "lm")), P("lib", "lm", "hit"))
    return jax.shard_map(
        local, mesh=mesh, in_specs=placed, out_specs=P(("lib", "hit"), "lm"), check_vma=False
    )
```

```python
import functools

import jax
import jax.numpy as jnp
from jax import lax
from jax.experimental import pallas as pl
from jax.experimental.pallas import tpu as pltpu
from jax.sharding import PartitionSpec as P

F8 = jnp.float8_e4m3fn
BITS = 16
VMEM = pl.BlockSpec(memory_space=pltpu.VMEM)
ANY = pl.BlockSpec(memory_space=pl.ANY)


def unpack_kernel(word_ref, bits_ref, count_ref):
    blocks, rows, width = word_ref.shape
    for at in range(blocks):
        here = slice(at * rows, (at + 1) * rows)
        words = word_ref[at].astype(jnp.int32)
        count = jnp.sum(lax.population_count(words).astype(jnp.float32), axis=1, keepdims=True)
        count_ref[here, :] = jnp.broadcast_to(count, (rows, count_ref.shape[1]))
        for bit in range(BITS):
            flag = ((words >> bit) & 1).astype(jnp.int8)
            bits_ref[here, bit * width : (bit + 1) * width] = flag.astype(F8)


def unpack(words):
    blocks, rows, width = words.shape
    return pl.pallas_call(
        unpack_kernel,
        in_specs=[VMEM],
        out_specs=[VMEM, VMEM],
        out_shape=[
            jax.ShapeDtypeStruct((blocks * rows, BITS * width), F8),
            jax.ShapeDtypeStruct((blocks * rows, 128), jnp.float32),
        ],
        compiler_params=pltpu.CompilerParams(vmem_limit_bytes=24 * 2**20),
        cost_estimate=pl.CostEstimate(flops=1, bytes_accessed=rows * width, transcendentals=0),
        name="unpack",
    )(words)


def spread_kernel(mine_ref, other_ref, own_ref, sib_ref, *refs, steps, hit_rows, chunk):
    out_ref = refs[-1]
    cols = own_ref.shape[1]
    half = mine_ref.shape[1]
    rows = hit_rows // 2
    side = lax.axis_index("lm")
    me = lax.axis_index("hit")
    parts = [
        lax.broadcasted_iota(jnp.int32, (rows, 1), 0) + ((me ^ k) * hit_rows + side * rows)
        for k in steps
    ]
    ids = jnp.concatenate(parts, axis=0)
    own = sib = None
    for place, pick_ref in ((side, mine_ref), (1 - side, other_ref)):
        for start in range(0, half, chunk):
            picks = pick_ref[0:1, start : start + chunk]
            hot = jnp.where(picks == ids, 1.0, 0.0).astype(jnp.bfloat16)
            at = pl.ds(pl.multiple_of(place * half + start, chunk), chunk)
            part = jnp.dot(hot, own_ref[at, :], preferred_element_type=jnp.float32)
            own = part if own is None else own + part
            part = jnp.dot(hot, sib_ref[at, :], preferred_element_type=jnp.float32)
            sib = part if sib is None else sib + part
    out_ref[:cols, :] = own.T.astype(jnp.bfloat16)
    out_ref[cols:, :] = sib.T.astype(jnp.bfloat16)


def spread(steps, hit_rows, mine, other, own, sib, after):
    marks, cols = own.shape
    hits = len(steps) * hit_rows // 2
    return pl.pallas_call(
        functools.partial(spread_kernel, steps=steps, hit_rows=hit_rows, chunk=512),
        in_specs=[VMEM] * 4 + [ANY] * len(after),
        out_specs=VMEM,
        out_shape=jax.ShapeDtypeStruct((2 * cols, hits), jnp.bfloat16),
        compiler_params=pltpu.CompilerParams(vmem_limit_bytes=24 * 2**20),
        cost_estimate=pl.CostEstimate(
            flops=marks * cols, bytes_accessed=marks * cols, transcendentals=0
        ),
        name="spread",
    )(mine, other, own, sib, *after)


def block_kernel(words_ref, *refs, which, sums, pairs, tile):
    flags, kern = refs[-2:]
    sum_refs = refs[:sums]
    pair_refs = refs[sums : sums + 2 * pairs]
    words = words_ref[which].astype(jnp.int32).T
    width = words.shape[0]
    count = jnp.sum(lax.population_count(words).astype(jnp.float32), axis=0, keepdims=True)
    for bit in range(BITS):
        flag = ((words >> bit) & 1).astype(jnp.int8)
        flags[bit * width : (bit + 1) * width, :] = flag.astype(F8)
    at = 0
    for bits_ref, count_ref in zip(pair_refs[::2], pair_refs[1::2]):
        rows = bits_ref.shape[0]
        size = min(tile, rows)
        for low in range(0, rows, size):
            here = slice(low, low + size)
            common = jnp.dot(bits_ref[here, :], flags[...], preferred_element_type=jnp.float32)
            union = (count + count_ref[here, 0:1]) - common
            kern[at : at + size, :] = (common / union).astype(jnp.bfloat16)
            at += size
    at = 0
    made = []
    for ref in sum_refs:
        rows = ref.shape[1]
        made.append(
            jnp.dot(ref[...], kern[at : at + rows, :], preferred_element_type=jnp.float32)
        )
        at += rows
    mine = sum(made[: sums // 2])
    theirs = sum(made[sums // 2 :])
    cols = mine.shape[0] // 2
    own = (mine[:cols] + theirs[cols:]).T.astype(jnp.bfloat16)
    sib = (mine[cols:] + theirs[:cols]).T.astype(jnp.bfloat16)
    if len(refs[:-2]) and len(refs[-3].shape) == 3:
        refs[-3][0] = own
        refs[-3][1] = sib
    else:
        refs[-4][...] = own
        refs[-3][...] = sib


def block(words, which, sums, pairs, after, split):
    _, rows, width = words.shape
    cols = sums[0].shape[0] // 2
    hits = sum(x.shape[1] for x in sums)
    flat = [x for pair in pairs for x in pair]
    one = jax.ShapeDtypeStruct((rows, cols), jnp.bfloat16)
    both = jax.ShapeDtypeStruct((2, rows, cols), jnp.bfloat16)
    return pl.pallas_call(
        functools.partial(block_kernel, which=which, sums=len(sums), pairs=len(pairs), tile=512),
        in_specs=[VMEM] * (1 + len(sums) + len(flat)) + [ANY] * len(after),
        out_specs=[VMEM, VMEM] if split else VMEM,
        out_shape=[one, one] if split else both,
        scratch_shapes=[
            pltpu.VMEM((BITS * width, rows), F8),
            pltpu.VMEM((hits, rows), jnp.bfloat16),
        ],
        compiler_params=pltpu.CompilerParams(vmem_limit_bytes=32 * 2**20),
        cost_estimate=pl.CostEstimate(
            flops=hits * rows, bytes_accessed=rows * cols, transcendentals=0
        ),
        name="block",
    )(words, *sums, *flat, *after)


def fill_kernel(*refs, steps):
    out_ref = refs[-1]
    side = lax.axis_index("lm")
    me = lax.axis_index("hit")
    for i, k in enumerate(steps):
        for at, which in ((0, side), (1, 1 - side)):
            ref = refs[2 * i + at]
            piece = ref[at] if len(ref.shape) == 3 else ref[...]
            rows, cols = piece.shape
            row = pl.ds(pl.multiple_of(which * rows, rows), rows)
            out_ref[row, pl.ds(pl.multiple_of((me ^ k) * cols, cols), cols)] = piece


def fill(steps, pieces, shape):
    return pl.pallas_call(
        functools.partial(fill_kernel, steps=steps),
        in_specs=[VMEM] * (2 * len(pieces)),
        out_specs=VMEM,
        out_shape=jax.ShapeDtypeStruct(shape, jnp.bfloat16),
        compiler_params=pltpu.CompilerParams(vmem_limit_bytes=16 * 2**20),
        name="fill",
    )(*[x for piece in pieces for x in piece])


def patch_kernel(own_ref, old_ref, out_ref, sems, *, step):
    side = lax.axis_index("lm")
    me = lax.axis_index("hit")
    copies = []
    for at, which in ((0, side), (1, 1 - side)):
        _, rows, cols = own_ref.shape
        row = pl.ds(pl.multiple_of(which * rows, rows), rows)
        col = pl.ds(pl.multiple_of((me ^ step) * cols, cols), cols)
        copies.append(pltpu.make_async_copy(own_ref.at[at], out_ref.at[row, col], sems.at[at]))
    for copy in copies:
        copy.start()
    for copy in copies:
        copy.wait()


def patch(step, piece, old):
    return pl.pallas_call(
        functools.partial(patch_kernel, step=step),
        in_specs=[VMEM, ANY],
        out_specs=ANY,
        out_shape=jax.ShapeDtypeStruct(old.shape, old.dtype),
        scratch_shapes=[pltpu.SemaphoreType.DMA((2,))],
        input_output_aliases={1: 0},
        name="patch",
    )(piece, old)


def small(fingerprints, pick_list, inverse_root):
    hit_rows, width = fingerprints.shape
    devices = lax.axis_size("hit")
    side = lax.axis_index("lm")
    half = hit_rows // 2
    weight = inverse_root[:, 0, :]
    cols = weight.shape[1]

    def across(x, k):
        return lax.ppermute(x, "hit", [(i, i ^ k) for i in range(devices)])

    def over(x):
        return lax.ppermute(x, "lm", [(0, 1), (1, 0)])

    mine = lax.dynamic_slice_in_dim(fingerprints, side * half, half).astype(jnp.uint16)
    other_picks = over(pick_list)
    other_weight = over(weight)

    even = list(range(0, devices, 2))
    odd = [k ^ 1 for k in even]
    words_even = jnp.stack([across(mine, k) if k else mine for k in even])
    words_odd = across(words_even, 1)

    args = (hit_rows, pick_list.reshape(1, -1), other_picks.reshape(1, -1), weight, other_weight)
    sums_even = spread(even, *args, [words_even])
    sums_odd = spread(odd, *args, [words_odd, sums_even])
    sums = [sums_even, sums_odd, over(sums_even), over(sums_odd)]
    pairs = [unpack(x) for x in (words_even, words_odd, over(words_even), over(words_odd))]

    far = list(range(devices - 1, devices // 2 - 1, -1))
    near = list(range(devices // 2 - 1, -1, -1))
    order = far[:2] + near[:1]
    for k, other in zip(far[2:], near[1:]):
        order += [k, other]
    order += [k for k in near if k not in order]
    last = far[-1]
    got = dict()
    sib = dict()
    made = []
    for at, k in enumerate(order):
        after = list(made)
        if k in far[2:]:
            after.append(got[far[far.index(k) - 2]])
        if at > order.index(last):
            after += [sib[x] for x in order[: 2 * (at - order.index(last))]]
        words = words_odd if k % 2 else words_even
        made = block(words, k // 2, sums, pairs, after, k == last)
        if k == last:
            made = jnp.stack([made[0], over(made[1])])
        got[k] = across(made, k) if k else made
        if k != last:
            sib[k] = over(got[k][1])
        made = [made]

    shape = (hit_rows, devices * cols)
    early = [k for k in order if k != last]
    return patch(last, got[last], fill(early, [(got[k], sib[k]) for k in early], shape))


def large(fingerprints, pick_list, inverse_root):
    hit_rows, width = fingerprints.shape
    devices = lax.axis_size("hit")
    side = lax.axis_index("lm")
    half = hit_rows // 2
    weight = inverse_root[:, 0, :]
    cols = weight.shape[1]
    picks = lax.all_gather(pick_list, "lm", tiled=True)
    words = lax.all_gather(fingerprints, "hit", tiled=True)
    hits = words.shape[0]
    blocks = words.reshape(devices, hit_rows, width)

    def spread_block(index):
        hot = (index * hit_rows + jnp.arange(hit_rows))[:, None] == picks[None, :]
        made = jnp.dot(hot.astype(jnp.bfloat16), weight, preferred_element_type=jnp.float32)
        return made.astype(jnp.bfloat16)

    def flag_block(block_words):
        flags = [((block_words >> bit) & 1).astype(F8) for bit in range(BITS)]
        return jnp.concatenate(flags, axis=1)

    sums = lax.map(spread_block, jnp.arange(devices)).reshape(hits, cols)
    sums = lax.all_gather(sums, "lm", axis=1, tiled=True)
    bits = lax.map(flag_block, blocks).reshape(hits, BITS * width)
    count = jnp.sum(lax.population_count(words), axis=1).astype(jnp.float32)

    def one(index):
        start = index * hit_rows + side * half
        rows = lax.dynamic_slice_in_dim(bits, start, half)
        common = lax.dot_general(
            rows, bits, (((1,), (1,)), ((), ())), preferred_element_type=jnp.float32
        )
        union = lax.dynamic_slice_in_dim(count, start, half)[:, None] + count[None, :] - common
        kernel = (common / union).astype(jnp.bfloat16)
        return jnp.dot(kernel, sums, preferred_element_type=jnp.float32).astype(jnp.bfloat16)

    made = lax.map(one, jnp.arange(devices))
    got = lax.all_to_all(made, "hit", 0, 0, tiled=True)
    got = got.reshape(devices, half, 2, cols).transpose(2, 1, 0, 3)
    got = got.reshape(2, 1, half, devices * cols)
    return lax.all_to_all(got, "lm", 0, 1, tiled=True).reshape(hit_rows, devices * cols)


def local(fingerprints, pick_list, inverse_root):
    if lax.axis_size("hit") > 8:
        return large(fingerprints, pick_list, inverse_root)
    return small(fingerprints, pick_list, inverse_root)


def solution(mesh):
    placed = (P(("lib", "hit"), None), P(("lib", "lm")), P("lib", "lm", "hit"))
    return jax.shard_map(
        local, mesh=mesh, in_specs=placed, out_specs=P(("lib", "hit"), "lm"), check_vma=False
    )
```

```python
import functools

import jax
import jax.numpy as jnp
from jax import lax
from jax.experimental import pallas as pl
from jax.experimental.pallas import tpu as pltpu
from jax.sharding import PartitionSpec as P

F8 = jnp.float8_e4m3fn
BITS = 16
VMEM = pl.BlockSpec(memory_space=pltpu.VMEM)
ANY = pl.BlockSpec(memory_space=pl.ANY)


def unpack_kernel(*refs, count, stack, single, inputs):
    bits_ref, count_ref = refs[inputs : inputs + 2]
    more = refs[inputs + 2 :]
    for at in range(count):
        block = refs[0][at] if len(refs[0].shape) == 3 else refs[at][...]
        rows, width = block.shape
        if stack:
            more[0][at] = block
        if single:
            more[at - count][...] = block
        here = slice(at * rows, (at + 1) * rows)
        words = block.astype(jnp.int32)
        ones = jnp.sum(lax.population_count(words).astype(jnp.float32), axis=1, keepdims=True)
        count_ref[here, :] = jnp.broadcast_to(ones, (rows, count_ref.shape[1]))
        for bit in range(BITS):
            flag = ((words >> bit) & 1).astype(jnp.int8)
            bits_ref[here, bit * width : (bit + 1) * width] = flag.astype(F8)


def unpack(words, after=(), stack=False, single=False):
    words = list(words) if isinstance(words, (list, tuple)) else [words]
    rows, width = words[0].shape[-2:]
    count = words[0].shape[0] if len(words[0].shape) == 3 else len(words)
    shapes = [
        jax.ShapeDtypeStruct((count * rows, BITS * width), F8),
        jax.ShapeDtypeStruct((count * rows, 128), jnp.float32),
    ]
    if stack:
        shapes.append(jax.ShapeDtypeStruct((count, rows, width), words[0].dtype))
    if single:
        shapes += [jax.ShapeDtypeStruct((rows, width), words[0].dtype)] * count
    out = pl.pallas_call(
        functools.partial(
            unpack_kernel,
            count=count,
            stack=stack,
            single=single,
            inputs=len(words) + len(after),
        ),
        in_specs=[VMEM] * len(words) + [ANY] * len(after),
        out_specs=[VMEM] * len(shapes),
        out_shape=shapes,
        compiler_params=pltpu.CompilerParams(vmem_limit_bytes=24 * 2**20),
        cost_estimate=pl.CostEstimate(
            flops=4096 * count * rows * BITS * width, bytes_accessed=rows * width, transcendentals=0
        ),
        name="unpack",
    )(*words, *after)
    return tuple(out[:2]), out[2:]


def spread_kernel(mine_ref, own_ref, other_ref, sib_ref, *refs, steps, hit_rows, chunk):
    out_ref = refs[-1]
    cols = own_ref.shape[1]
    half = mine_ref.shape[1]
    rows = hit_rows // 2
    side = lax.axis_index("lm")
    me = lax.axis_index("hit")
    places = []
    for place in (side, 1 - side):
        for start in range(0, half, chunk):
            at = pl.ds(pl.multiple_of(place * half + start, chunk), chunk)
            places.append((start, at))
    parts = [
        lax.broadcasted_iota(jnp.int32, (rows, 1), 0) + ((me ^ k) * hit_rows + side * rows)
        for k in steps
    ]
    ids = jnp.concatenate(parts, axis=0)
    own = sib = None
    for i, (start, at) in enumerate(places):
        pick_ref = mine_ref if i < len(places) // 2 else other_ref
        hot = jnp.where(pick_ref[0:1, start : start + chunk] == ids, 1.0, 0.0).astype(jnp.bfloat16)
        part = jnp.dot(hot, sib_ref[at, :], preferred_element_type=jnp.float32)
        sib = part if sib is None else sib + part
        part = jnp.dot(hot, own_ref[at, :], preferred_element_type=jnp.float32)
        own = part if own is None else own + part
    out_ref[:cols, :] = own.T.astype(jnp.bfloat16)
    out_ref[cols:, :] = sib.T.astype(jnp.bfloat16)


def spread(steps, hit_rows, mine, own, other, sib, after):
    marks, cols = own.shape
    hits = len(steps) * hit_rows // 2
    chunk = 512
    return pl.pallas_call(
        functools.partial(spread_kernel, steps=steps, hit_rows=hit_rows, chunk=chunk),
        in_specs=[VMEM] * 4 + [ANY] * len(after),
        out_specs=VMEM,
        out_shape=jax.ShapeDtypeStruct((2 * cols, hits), jnp.bfloat16),
        compiler_params=pltpu.CompilerParams(vmem_limit_bytes=24 * 2**20),
        cost_estimate=pl.CostEstimate(
            flops=marks * cols * hits // 8, bytes_accessed=marks * cols, transcendentals=0
        ),
        name="spread",
    )(mine, own, other, sib, *after)


def block_kernel(words_ref, *refs, sums, pairs, tile):
    later_ref, both_ref, own_ref, sib_ref, flags, kern = refs[-6:]
    sum_refs = refs[:sums]
    pair_refs = refs[sums : sums + 2 * pairs]
    held = refs[sums + 2 * pairs : sums + 2 * pairs + 2]
    later_ref[0] = held[0][...]
    later_ref[1] = held[1][...]
    words = words_ref[...].astype(jnp.int32).T
    width = words.shape[0]
    count = jnp.sum(lax.population_count(words).astype(jnp.float32), axis=0, keepdims=True)
    for bit in range(BITS):
        flag = ((words >> bit) & 1).astype(jnp.int8)
        flags[bit * width : (bit + 1) * width, :] = flag.astype(F8)
    at = 0
    for bits_ref, count_ref in zip(pair_refs[::2], pair_refs[1::2]):
        rows = bits_ref.shape[0]
        size = min(tile, rows)
        for low in range(0, rows, size):
            here = slice(low, low + size)
            common = jnp.dot(bits_ref[here, :], flags[...], preferred_element_type=jnp.float32)
            union = (count + count_ref[here, 0:1]) - common
            kern[at : at + size, :] = (common / union).astype(jnp.bfloat16)
            at += size
    at = 0
    made = []
    for ref in sum_refs:
        rows = ref.shape[1]
        made.append(
            jnp.dot(ref[...], kern[at : at + rows, :], preferred_element_type=jnp.float32)
        )
        at += rows
    mine = sum(made[: sums // 2])
    theirs = sum(made[sums // 2 :])
    cols = mine.shape[0] // 2
    own = (mine[:cols] + theirs[cols:]).T.astype(jnp.bfloat16)
    sib = (mine[cols:] + theirs[:cols]).T.astype(jnp.bfloat16)
    both_ref[0] = own
    both_ref[1] = sib
    own_ref[...] = own
    sib_ref[...] = sib


def block(words, sums, pairs, held, after):
    rows, width = words.shape
    cols = sums[0].shape[0] // 2
    hits = sum(x.shape[1] for x in sums)
    flat = [x for pair in pairs for x in pair] + list(held)
    one = jax.ShapeDtypeStruct((rows, cols), jnp.bfloat16)
    both = jax.ShapeDtypeStruct((2, rows, cols), jnp.bfloat16)
    return pl.pallas_call(
        functools.partial(block_kernel, sums=len(sums), pairs=len(pairs), tile=512),
        in_specs=[VMEM] * (1 + len(sums) + len(flat)) + [ANY] * len(after),
        out_specs=[VMEM] * 4,
        out_shape=[both, both, one, one],
        scratch_shapes=[
            pltpu.VMEM((BITS * width, rows), F8),
            pltpu.VMEM((hits, rows), jnp.bfloat16),
        ],
        compiler_params=pltpu.CompilerParams(vmem_limit_bytes=32 * 2**20),
        cost_estimate=pl.CostEstimate(
            flops=2 * hits * rows * (BITS * width + 2 * cols),
            bytes_accessed=rows * cols,
            transcendentals=0,
        ),
        name="block",
    )(words, *sums, *flat, *after)


def fill_kernel(*refs, steps):
    out_ref = refs[-1]
    side = lax.axis_index("lm")
    me = lax.axis_index("hit")
    for i, k in enumerate(steps):
        for at, which in ((0, side), (1, 1 - side)):
            ref = refs[2 * i + at]
            piece = ref[at] if len(ref.shape) == 3 else ref[...]
            rows, cols = piece.shape
            row = pl.ds(pl.multiple_of(which * rows, rows), rows)
            out_ref[row, pl.ds(pl.multiple_of((me ^ k) * cols, cols), cols)] = piece


def fill(steps, pieces, shape, after):
    return pl.pallas_call(
        functools.partial(fill_kernel, steps=steps),
        in_specs=[VMEM] * (2 * len(pieces)) + [ANY] * len(after),
        out_specs=VMEM,
        out_shape=jax.ShapeDtypeStruct(shape, jnp.bfloat16),
        compiler_params=pltpu.CompilerParams(vmem_limit_bytes=16 * 2**20),
        name="fill",
    )(*[x for piece in pieces for x in piece], *after)


def small(fingerprints, pick_list, inverse_root):
    hit_rows, width = fingerprints.shape
    devices = lax.axis_size("hit")
    side = lax.axis_index("lm")
    half = hit_rows // 2
    weight = inverse_root[:, 0, :]
    cols = weight.shape[1]

    def across(x, k):
        return lax.ppermute(x, "hit", [(i, i ^ k) for i in range(devices)])

    def over(x):
        return lax.ppermute(x, "lm", [(0, 1), (1, 0)])

    mine = lax.dynamic_slice_in_dim(fingerprints, side * half, half).astype(jnp.uint16)
    other_picks = over(pick_list)
    other_weight = over(weight)

    even = list(range(0, devices, 2))
    odd = [k ^ 1 for k in even]
    words_z = [across(mine, k) if k else mine for k in even]

    args = (hit_rows, pick_list.reshape(1, -1), weight, other_picks.reshape(1, -1), other_weight)
    sums = [spread(even, *args, [])]
    pair_even, (words_even, *list_even) = unpack(words_z, sums, True, True)
    words_odd = across(words_even, 1)
    sums.append(spread(odd, *args, [words_even]))
    sums += [over(x) for x in sums]
    pair_odd, list_odd = unpack(words_odd, single=True)
    pairs = [pair_even, pair_odd, unpack(over(words_even))[0], unpack(over(words_odd))[0]]
    words = dict(zip(even + odd, [*list_even, *list_odd]))

    order = list(range(devices - 1, -1, -1))
    direct, hands, waits = order[:-1], {}, {}
    if devices == 8:
        order = [7, 6, 4, 5, 3, 2, 1, 0]
        direct = [7, 6, 5, 3, 2, 1]
        hands = {3: 4}
        waits = {2: [7], 1: [6]}
    halves = dict()
    pieces = dict()
    got = dict()
    out = (sums[0],) * 4
    held = (sums[0][:half, :cols],) * 2
    for k in order:
        after = list(out) + [got[x] for x in waits.get(k, [])]
        after += [out[0]] * (6 - len(after))
        if k in hands:
            held = halves[hands[k]]
        later, made, *last = out = block(words[k], sums, pairs, held, after)
        held = last
        if k in hands:
            x = hands[k]
            got[x] = across(later, x)
            pieces[x] = (got[x], got[x])
        if k in direct:
            got[k] = across(made, k)
            pieces[k] = (got[k], over(got[k][1]))
        else:
            halves[k] = (last[0], over(last[1]))
    pieces[0] = halves[0]
    return fill(order, [pieces[k] for k in order], (hit_rows, devices * cols), out[:2])


def large(fingerprints, pick_list, inverse_root):
    hit_rows, width = fingerprints.shape
    devices = lax.axis_size("hit")
    side = lax.axis_index("lm")
    half = hit_rows // 2
    weight = inverse_root[:, 0, :]
    cols = weight.shape[1]
    picks = lax.all_gather(pick_list, "lm", tiled=True)
    words = lax.all_gather(fingerprints, "hit", tiled=True)
    hits = words.shape[0]
    blocks = words.reshape(devices, hit_rows, width)

    def spread_block(index):
        hot = (index * hit_rows + jnp.arange(hit_rows))[:, None] == picks[None, :]
        made = jnp.dot(hot.astype(jnp.bfloat16), weight, preferred_element_type=jnp.float32)
        return made.astype(jnp.bfloat16)

    def flag_block(block_words):
        flags = [((block_words >> bit) & 1).astype(F8) for bit in range(BITS)]
        return jnp.concatenate(flags, axis=1)

    sums = lax.map(spread_block, jnp.arange(devices)).reshape(hits, cols)
    sums = lax.all_gather(sums, "lm", axis=1, tiled=True)
    bits = lax.map(flag_block, blocks).reshape(hits, BITS * width)
    count = jnp.sum(lax.population_count(words), axis=1).astype(jnp.float32)

    def one(index):
        start = index * hit_rows + side * half
        rows = lax.dynamic_slice_in_dim(bits, start, half)
        common = lax.dot_general(
            rows, bits, (((1,), (1,)), ((), ())), preferred_element_type=jnp.float32
        )
        union = lax.dynamic_slice_in_dim(count, start, half)[:, None] + count[None, :] - common
        kernel = (common / union).astype(jnp.bfloat16)
        return jnp.dot(kernel, sums, preferred_element_type=jnp.float32).astype(jnp.bfloat16)

    made = lax.map(one, jnp.arange(devices))
    got = lax.all_to_all(made, "hit", 0, 0, tiled=True)
    got = got.reshape(devices, half, 2, cols).transpose(2, 1, 0, 3)
    got = got.reshape(2, 1, half, devices * cols)
    return lax.all_to_all(got, "lm", 0, 1, tiled=True).reshape(hit_rows, devices * cols)


def local(fingerprints, pick_list, inverse_root):
    if lax.axis_size("hit") > 8:
        return large(fingerprints, pick_list, inverse_root)
    return small(fingerprints, pick_list, inverse_root)


def solution(mesh):
    placed = (P(("lib", "hit"), None), P(("lib", "lm")), P("lib", "lm", "hit"))
    return jax.shard_map(
        local, mesh=mesh, in_specs=placed, out_specs=P(("lib", "hit"), "lm"), check_vma=False
    )
```

```python
import functools

import jax
import jax.numpy as jnp
from jax import lax
from jax.experimental import pallas as pl
from jax.experimental.pallas import tpu as pltpu
from jax.sharding import PartitionSpec as P

F8 = jnp.float8_e4m3fn
BITS = 16
VMEM = pl.BlockSpec(memory_space=pltpu.VMEM)
ANY = pl.BlockSpec(memory_space=pl.ANY)


def unpack_kernel(*refs, count, stack, single, inputs):
    bits_ref, count_ref = refs[inputs : inputs + 2]
    more = refs[inputs + 2 :]
    word_ref = refs[0]
    if stack:
        word_ref = more[0]
        for at in range(count):
            word_ref[at] = refs[at][...]
    if single:
        for at in range(count):
            more[at - count][...] = word_ref[at]

    @pl.loop(0, count)
    def _(at):
        words = word_ref[at].astype(jnp.int32)
        rows, width = words.shape
        here = pl.ds(pl.multiple_of(at * rows, rows), rows)
        ones = jnp.sum(lax.population_count(words).astype(jnp.float32), axis=1, keepdims=True)
        count_ref[here, :] = jnp.broadcast_to(ones, (rows, count_ref.shape[1]))
        for bit in range(BITS):
            flag = ((words >> bit) & 1).astype(jnp.int8)
            bits_ref[here, bit * width : (bit + 1) * width] = flag.astype(F8)


def unpack(words, after=(), stack=False, single=False):
    words = list(words) if isinstance(words, (list, tuple)) else [words]
    rows, width = words[0].shape[-2:]
    count = words[0].shape[0] if len(words[0].shape) == 3 else len(words)
    shapes = [
        jax.ShapeDtypeStruct((count * rows, BITS * width), F8),
        jax.ShapeDtypeStruct((count * rows, 128), jnp.float32),
    ]
    if stack:
        shapes.append(jax.ShapeDtypeStruct((count, rows, width), words[0].dtype))
    if single:
        shapes += [jax.ShapeDtypeStruct((rows, width), words[0].dtype)] * count
    out = pl.pallas_call(
        functools.partial(
            unpack_kernel,
            count=count,
            stack=stack,
            single=single,
            inputs=len(words) + len(after),
        ),
        in_specs=[VMEM] * len(words) + [ANY] * len(after),
        out_specs=[VMEM] * len(shapes),
        out_shape=shapes,
        compiler_params=pltpu.CompilerParams(vmem_limit_bytes=24 * 2**20),
        cost_estimate=pl.CostEstimate(
            flops=4096 * count * rows * BITS * width, bytes_accessed=rows * width, transcendentals=0
        ),
        name="unpack",
    )(*words, *after)
    return tuple(out[:2]), out[2:]


def spread_kernel(mine_ref, own_ref, other_ref, sib_ref, *refs, steps, hit_rows, chunk):
    out_ref = refs[-1]
    cols = own_ref.shape[1]
    half = mine_ref.shape[1]
    rows = hit_rows // 2
    side = lax.axis_index("lm")
    me = lax.axis_index("hit")
    places = []
    for place in (side, 1 - side):
        for start in range(0, half, chunk):
            at = pl.ds(pl.multiple_of(place * half + start, chunk), chunk)
            places.append((start, at))
    parts = [
        lax.broadcasted_iota(jnp.int32, (rows, 1), 0) + ((me ^ k) * hit_rows + side * rows)
        for k in steps
    ]
    ids = jnp.concatenate(parts, axis=0)
    own = sib = None
    for i, (start, at) in enumerate(places):
        pick_ref = mine_ref if i < len(places) // 2 else other_ref
        hot = jnp.where(pick_ref[0:1, start : start + chunk] == ids, 1.0, 0.0).astype(jnp.bfloat16)
        part = jnp.dot(hot, sib_ref[at, :], preferred_element_type=jnp.float32)
        sib = part if sib is None else sib + part
        part = jnp.dot(hot, own_ref[at, :], preferred_element_type=jnp.float32)
        own = part if own is None else own + part
    out_ref[:cols, :] = own.T.astype(jnp.bfloat16)
    out_ref[cols:, :] = sib.T.astype(jnp.bfloat16)


def spread(steps, hit_rows, mine, own, other, sib, after):
    marks, cols = own.shape
    hits = len(steps) * hit_rows // 2
    chunk = 512
    return pl.pallas_call(
        functools.partial(spread_kernel, steps=steps, hit_rows=hit_rows, chunk=chunk),
        in_specs=[VMEM] * 4 + [ANY] * len(after),
        out_specs=VMEM,
        out_shape=jax.ShapeDtypeStruct((2 * cols, hits), jnp.bfloat16),
        compiler_params=pltpu.CompilerParams(vmem_limit_bytes=24 * 2**20),
        cost_estimate=pl.CostEstimate(
            flops=marks * cols * hits // 8, bytes_accessed=marks * cols, transcendentals=0
        ),
        name="spread",
    )(mine, own, other, sib, *after)


def block_kernel(words_ref, *refs, sums, pairs, tile):
    later_ref, both_ref, own_ref, sib_ref, flags, kern = refs[-6:]
    sum_refs = refs[:sums]
    pair_refs = refs[sums : sums + 2 * pairs]
    held = refs[sums + 2 * pairs : sums + 2 * pairs + 2]
    later_ref[0] = held[0][...]
    later_ref[1] = held[1][...]
    words = words_ref[...].astype(jnp.int32).T
    width = words.shape[0]
    count = jnp.sum(lax.population_count(words).astype(jnp.float32), axis=0, keepdims=True)
    for bit in range(BITS):
        flag = ((words >> bit) & 1).astype(jnp.int8)
        flags[bit * width : (bit + 1) * width, :] = flag.astype(F8)
    at = 0
    for bits_ref, count_ref in zip(pair_refs[::2], pair_refs[1::2]):
        rows = bits_ref.shape[0]
        size = min(tile, rows)
        for low in range(0, rows, size):
            here = slice(low, low + size)
            common = jnp.dot(bits_ref[here, :], flags[...], preferred_element_type=jnp.float32)
            union = (count + count_ref[here, 0:1]) - common
            kern[at : at + size, :] = (common / union).astype(jnp.bfloat16)
            at += size
    at = 0
    made = []
    for ref in sum_refs:
        rows = ref.shape[1]
        made.append(
            jnp.dot(ref[...], kern[at : at + rows, :], preferred_element_type=jnp.float32)
        )
        at += rows
    mine = sum(made[: sums // 2])
    theirs = sum(made[sums // 2 :])
    cols = mine.shape[0] // 2
    own = (mine[:cols] + theirs[cols:]).T.astype(jnp.bfloat16)
    sib = (mine[cols:] + theirs[:cols]).T.astype(jnp.bfloat16)
    both_ref[0] = own
    both_ref[1] = sib
    own_ref[...] = own
    sib_ref[...] = sib


def block(words, sums, pairs, held, after):
    rows, width = words.shape
    cols = sums[0].shape[0] // 2
    hits = sum(x.shape[1] for x in sums)
    flat = [x for pair in pairs for x in pair] + list(held)
    one = jax.ShapeDtypeStruct((rows, cols), jnp.bfloat16)
    both = jax.ShapeDtypeStruct((2, rows, cols), jnp.bfloat16)
    return pl.pallas_call(
        functools.partial(block_kernel, sums=len(sums), pairs=len(pairs), tile=512),
        in_specs=[VMEM] * (1 + len(sums) + len(flat)) + [ANY] * len(after),
        out_specs=[VMEM] * 4,
        out_shape=[both, both, one, one],
        scratch_shapes=[
            pltpu.VMEM((BITS * width, rows), F8),
            pltpu.VMEM((hits, rows), jnp.bfloat16),
        ],
        compiler_params=pltpu.CompilerParams(vmem_limit_bytes=32 * 2**20),
        cost_estimate=pl.CostEstimate(
            flops=2 * hits * rows * (BITS * width + 2 * cols),
            bytes_accessed=rows * cols,
            transcendentals=0,
        ),
        name="block",
    )(words, *sums, *flat, *after)


def fill_kernel(*refs, steps):
    out_ref = refs[-1]
    side = lax.axis_index("lm")
    me = lax.axis_index("hit")
    for i, k in enumerate(steps):
        for at, which in ((0, side), (1, 1 - side)):
            ref = refs[2 * i + at]
            piece = ref[at] if len(ref.shape) == 3 else ref[...]
            rows, cols = piece.shape
            row = pl.ds(pl.multiple_of(which * rows, rows), rows)
            out_ref[row, pl.ds(pl.multiple_of((me ^ k) * cols, cols), cols)] = piece


def fill(steps, pieces, shape, after):
    return pl.pallas_call(
        functools.partial(fill_kernel, steps=steps),
        in_specs=[VMEM] * (2 * len(pieces)) + [ANY] * len(after),
        out_specs=VMEM,
        out_shape=jax.ShapeDtypeStruct(shape, jnp.bfloat16),
        compiler_params=pltpu.CompilerParams(vmem_limit_bytes=16 * 2**20),
        name="fill",
    )(*[x for piece in pieces for x in piece], *after)


def small(fingerprints, pick_list, inverse_root):
    hit_rows, width = fingerprints.shape
    devices = lax.axis_size("hit")
    side = lax.axis_index("lm")
    half = hit_rows // 2
    weight = inverse_root[:, 0, :]
    cols = weight.shape[1]

    def across(x, k):
        return lax.ppermute(x, "hit", [(i, i ^ k) for i in range(devices)])

    def over(x):
        return lax.ppermute(x, "lm", [(0, 1), (1, 0)])

    mine = lax.dynamic_slice_in_dim(fingerprints, side * half, half).astype(jnp.uint16)
    other_picks = over(pick_list)
    other_weight = over(weight)

    even = list(range(0, devices, 2))
    odd = [k ^ 1 for k in even]
    words_z = [across(mine, k) if k else mine for k in even]

    args = (hit_rows, pick_list.reshape(1, -1), weight, other_picks.reshape(1, -1), other_weight)
    sums = [spread(even, *args, [])]
    pair_even, (words_even, *list_even) = unpack(words_z, sums, True, True)
    words_odd = across(words_even, 1)
    sums.append(spread(odd, *args, [words_even]))
    sums += [over(x) for x in sums]
    pair_odd, list_odd = unpack(words_odd, single=True)
    pairs = [pair_even, pair_odd, unpack(over(words_even))[0], unpack(over(words_odd))[0]]
    words = dict(zip(even + odd, [*list_even, *list_odd]))

    order = list(range(devices - 1, -1, -1))
    direct, hands, waits = order[:-1], {}, {}
    if devices == 8:
        order = [7, 6, 4, 5, 3, 2, 1, 0]
        direct = [7, 6, 5, 3, 2, 1]
        hands = {3: 4}
        waits = {2: [7], 1: [6]}
    halves = dict()
    pieces = dict()
    got = dict()
    out = (sums[0],) * 4
    held = (sums[0][:half, :cols],) * 2
    for k in order:
        after = list(out) + [got[x] for x in waits.get(k, [])]
        after += [out[0]] * (6 - len(after))
        if k in hands:
            held = halves[hands[k]]
        later, made, *last = out = block(words[k], sums, pairs, held, after)
        held = last
        if k in hands:
            x = hands[k]
            got[x] = across(later, x)
            pieces[x] = (got[x], got[x])
        if k in direct:
            got[k] = across(made, k)
            pieces[k] = (got[k], over(got[k][1]))
        else:
            halves[k] = (last[0], over(last[1]))
    pieces[0] = halves[0]
    return fill(order, [pieces[k] for k in order], (hit_rows, devices * cols), out[:2])


def large(fingerprints, pick_list, inverse_root):
    hit_rows, width = fingerprints.shape
    devices = lax.axis_size("hit")
    side = lax.axis_index("lm")
    half = hit_rows // 2
    weight = inverse_root[:, 0, :]
    cols = weight.shape[1]
    picks = lax.all_gather(pick_list, "lm", tiled=True)
    words = lax.all_gather(fingerprints, "hit", tiled=True)
    hits = words.shape[0]
    blocks = words.reshape(devices, hit_rows, width)

    def spread_block(index):
        hot = (index * hit_rows + jnp.arange(hit_rows))[:, None] == picks[None, :]
        made = jnp.dot(hot.astype(jnp.bfloat16), weight, preferred_element_type=jnp.float32)
        return made.astype(jnp.bfloat16)

    def flag_block(block_words):
        flags = [((block_words >> bit) & 1).astype(F8) for bit in range(BITS)]
        return jnp.concatenate(flags, axis=1)

    sums = lax.map(spread_block, jnp.arange(devices)).reshape(hits, cols)
    sums = lax.all_gather(sums, "lm", axis=1, tiled=True)
    bits = lax.map(flag_block, blocks).reshape(hits, BITS * width)
    count = jnp.sum(lax.population_count(words), axis=1).astype(jnp.float32)

    def one(index):
        start = index * hit_rows + side * half
        rows = lax.dynamic_slice_in_dim(bits, start, half)
        common = lax.dot_general(
            rows, bits, (((1,), (1,)), ((), ())), preferred_element_type=jnp.float32
        )
        union = lax.dynamic_slice_in_dim(count, start, half)[:, None] + count[None, :] - common
        kernel = (common / union).astype(jnp.bfloat16)
        return jnp.dot(kernel, sums, preferred_element_type=jnp.float32).astype(jnp.bfloat16)

    made = lax.map(one, jnp.arange(devices))
    got = lax.all_to_all(made, "hit", 0, 0, tiled=True)
    got = got.reshape(devices, half, 2, cols).transpose(2, 1, 0, 3)
    got = got.reshape(2, 1, half, devices * cols)
    return lax.all_to_all(got, "lm", 0, 1, tiled=True).reshape(hit_rows, devices * cols)


def local(fingerprints, pick_list, inverse_root):
    if lax.axis_size("hit") > 8:
        return large(fingerprints, pick_list, inverse_root)
    return small(fingerprints, pick_list, inverse_root)


def solution(mesh):
    placed = (P(("lib", "hit"), None), P(("lib", "lm")), P("lib", "lm", "hit"))
    return jax.shard_map(
        local, mesh=mesh, in_specs=placed, out_specs=P(("lib", "hit"), "lm"), check_vma=False
    )
```

```python
import functools

import jax
import jax.numpy as jnp
from jax import lax
from jax.experimental import pallas as pl
from jax.experimental.pallas import tpu as pltpu
from jax.sharding import PartitionSpec as P

F8 = jnp.float8_e4m3fn
BITS = 16
VMEM = pl.BlockSpec(memory_space=pltpu.VMEM)
ANY = pl.BlockSpec(memory_space=pl.ANY)


def unpack_kernel(*refs, count, stack, single, inputs):
    bits_ref, count_ref = refs[inputs : inputs + 2]
    more = refs[inputs + 2 :]
    word_ref = refs[0]
    if stack:
        word_ref = more[0]
        for at in range(count):
            word_ref[at] = refs[at][...]
    if single:
        for at in range(count):
            more[at - count][...] = word_ref[at]

    @pl.loop(0, count, unroll=2)
    def _(at):
        words = word_ref[at].astype(jnp.int32)
        rows, width = words.shape
        here = pl.ds(pl.multiple_of(at * rows, rows), rows)
        ones = jnp.sum(lax.population_count(words).astype(jnp.float32), axis=1, keepdims=True)
        count_ref[here, :] = jnp.broadcast_to(ones, (rows, count_ref.shape[1]))
        for bit in range(BITS):
            flag = ((words >> bit) & 1).astype(jnp.int8)
            bits_ref[here, bit * width : (bit + 1) * width] = flag.astype(F8)


def unpack(words, after=(), stack=False, single=False):
    words = list(words) if isinstance(words, (list, tuple)) else [words]
    rows, width = words[0].shape[-2:]
    count = words[0].shape[0] if len(words[0].shape) == 3 else len(words)
    shapes = [
        jax.ShapeDtypeStruct((count * rows, BITS * width), F8),
        jax.ShapeDtypeStruct((count * rows, 128), jnp.float32),
    ]
    if stack:
        shapes.append(jax.ShapeDtypeStruct((count, rows, width), words[0].dtype))
    if single:
        shapes += [jax.ShapeDtypeStruct((rows, width), words[0].dtype)] * count
    out = pl.pallas_call(
        functools.partial(
            unpack_kernel,
            count=count,
            stack=stack,
            single=single,
            inputs=len(words) + len(after),
        ),
        in_specs=[VMEM] * len(words) + [ANY] * len(after),
        out_specs=[VMEM] * len(shapes),
        out_shape=shapes,
        compiler_params=pltpu.CompilerParams(vmem_limit_bytes=24 * 2**20),
        cost_estimate=pl.CostEstimate(
            flops=4096 * count * rows * BITS * width, bytes_accessed=rows * width, transcendentals=0
        ),
        name="unpack",
    )(*words, *after)
    return tuple(out[:2]), out[2:]


def spread_kernel(mine_ref, own_ref, other_ref, sib_ref, *refs, steps, hit_rows, chunk):
    out_ref = refs[-1]
    cols = own_ref.shape[1]
    half = mine_ref.shape[1]
    rows = hit_rows // 2
    side = lax.axis_index("lm")
    me = lax.axis_index("hit")
    places = []
    for place in (side, 1 - side):
        for start in range(0, half, chunk):
            at = pl.ds(pl.multiple_of(place * half + start, chunk), chunk)
            places.append((start, at))
    parts = [
        lax.broadcasted_iota(jnp.int32, (rows, 1), 0) + ((me ^ k) * hit_rows + side * rows)
        for k in steps
    ]
    ids = jnp.concatenate(parts, axis=0)
    own = sib = None
    for i, (start, at) in enumerate(places):
        pick_ref = mine_ref if i < len(places) // 2 else other_ref
        hot = jnp.where(pick_ref[0:1, start : start + chunk] == ids, 1.0, 0.0).astype(jnp.bfloat16)
        part = jnp.dot(hot, sib_ref[at, :], preferred_element_type=jnp.float32)
        sib = part if sib is None else sib + part
        part = jnp.dot(hot, own_ref[at, :], preferred_element_type=jnp.float32)
        own = part if own is None else own + part
    out_ref[:cols, :] = own.T.astype(jnp.bfloat16)
    out_ref[cols:, :] = sib.T.astype(jnp.bfloat16)


def spread(steps, hit_rows, mine, own, other, sib, after):
    marks, cols = own.shape
    hits = len(steps) * hit_rows // 2
    chunk = 512
    return pl.pallas_call(
        functools.partial(spread_kernel, steps=steps, hit_rows=hit_rows, chunk=chunk),
        in_specs=[VMEM] * 4 + [ANY] * len(after),
        out_specs=VMEM,
        out_shape=jax.ShapeDtypeStruct((2 * cols, hits), jnp.bfloat16),
        compiler_params=pltpu.CompilerParams(vmem_limit_bytes=24 * 2**20),
        cost_estimate=pl.CostEstimate(
            flops=marks * cols * hits // 8, bytes_accessed=marks * cols, transcendentals=0
        ),
        name="spread",
    )(mine, own, other, sib, *after)


def block_kernel(words_ref, *refs, sums, pairs, tile):
    later_ref, both_ref, own_ref, sib_ref, flags, kern = refs[-6:]
    sum_refs = refs[:sums]
    pair_refs = refs[sums : sums + 2 * pairs]
    held = refs[sums + 2 * pairs : sums + 2 * pairs + 2]
    later_ref[0] = held[0][...]
    later_ref[1] = held[1][...]
    words = words_ref[...].astype(jnp.int32).T
    width = words.shape[0]
    count = jnp.sum(lax.population_count(words).astype(jnp.float32), axis=0, keepdims=True)
    for bit in range(BITS):
        flag = ((words >> bit) & 1).astype(jnp.int8)
        flags[bit * width : (bit + 1) * width, :] = flag.astype(F8)
    at = 0
    for bits_ref, count_ref in zip(pair_refs[::2], pair_refs[1::2]):
        rows = bits_ref.shape[0]
        size = min(tile, rows)
        for low in range(0, rows, size):
            here = slice(low, low + size)
            common = jnp.dot(bits_ref[here, :], flags[...], preferred_element_type=jnp.float32)
            union = (count + count_ref[here, 0:1]) - common
            kern[at : at + size, :] = (common / union).astype(jnp.bfloat16)
            at += size
    at = 0
    made = []
    for ref in sum_refs:
        rows = ref.shape[1]
        made.append(
            jnp.dot(ref[...], kern[at : at + rows, :], preferred_element_type=jnp.float32)
        )
        at += rows
    mine = sum(made[: sums // 2])
    theirs = sum(made[sums // 2 :])
    cols = mine.shape[0] // 2
    own = (mine[:cols] + theirs[cols:]).T.astype(jnp.bfloat16)
    sib = (mine[cols:] + theirs[:cols]).T.astype(jnp.bfloat16)
    both_ref[0] = own
    both_ref[1] = sib
    own_ref[...] = own
    sib_ref[...] = sib


def block(words, sums, pairs, held, after):
    rows, width = words.shape
    cols = sums[0].shape[0] // 2
    hits = sum(x.shape[1] for x in sums)
    flat = [x for pair in pairs for x in pair] + list(held)
    one = jax.ShapeDtypeStruct((rows, cols), jnp.bfloat16)
    both = jax.ShapeDtypeStruct((2, rows, cols), jnp.bfloat16)
    return pl.pallas_call(
        functools.partial(block_kernel, sums=len(sums), pairs=len(pairs), tile=512),
        in_specs=[VMEM] * (1 + len(sums) + len(flat)) + [ANY] * len(after),
        out_specs=[VMEM] * 4,
        out_shape=[both, both, one, one],
        scratch_shapes=[
            pltpu.VMEM((BITS * width, rows), F8),
            pltpu.VMEM((hits, rows), jnp.bfloat16),
        ],
        compiler_params=pltpu.CompilerParams(vmem_limit_bytes=32 * 2**20),
        cost_estimate=pl.CostEstimate(
            flops=2 * hits * rows * (BITS * width + 2 * cols),
            bytes_accessed=rows * cols,
            transcendentals=0,
        ),
        name="block",
    )(words, *sums, *flat, *after)


def fill_kernel(*refs, steps):
    out_ref = refs[-1]
    side = lax.axis_index("lm")
    me = lax.axis_index("hit")
    rows, cols = refs[1].shape[-2:]
    band = rows // 4

    @pl.loop(0, rows // band)
    def _(step):
        low = pl.multiple_of(step * band, band)
        for i, k in enumerate(steps):
            for at, which in ((0, side), (1, 1 - side)):
                ref = refs[2 * i + at]
                here = pl.ds(low, band)
                piece = ref[at, here, :] if len(ref.shape) == 3 else ref[here, :]
                row = pl.ds(pl.multiple_of(which * rows + low, band), band)
                out_ref[row, pl.ds(pl.multiple_of((me ^ k) * cols, cols), cols)] = piece


def fill(steps, pieces, shape, after):
    return pl.pallas_call(
        functools.partial(fill_kernel, steps=steps),
        in_specs=[VMEM] * (2 * len(pieces)) + [ANY] * len(after),
        out_specs=VMEM,
        out_shape=jax.ShapeDtypeStruct(shape, jnp.bfloat16),
        compiler_params=pltpu.CompilerParams(vmem_limit_bytes=16 * 2**20),
        name="fill",
    )(*[x for piece in pieces for x in piece], *after)


def small(fingerprints, pick_list, inverse_root):
    hit_rows, width = fingerprints.shape
    devices = lax.axis_size("hit")
    side = lax.axis_index("lm")
    half = hit_rows // 2
    weight = inverse_root[:, 0, :]
    cols = weight.shape[1]

    def across(x, k):
        return lax.ppermute(x, "hit", [(i, i ^ k) for i in range(devices)])

    def over(x):
        return lax.ppermute(x, "lm", [(0, 1), (1, 0)])

    mine = lax.dynamic_slice_in_dim(fingerprints, side * half, half).astype(jnp.uint16)
    other_picks = over(pick_list)
    other_weight = over(weight)

    even = list(range(0, devices, 2))
    odd = [k ^ 1 for k in even]
    words_z = [across(mine, k) if k else mine for k in even]

    args = (hit_rows, pick_list.reshape(1, -1), weight, other_picks.reshape(1, -1), other_weight)
    sums = [spread(even, *args, [])]
    pair_even, (words_even, *list_even) = unpack(words_z, sums, True, True)
    words_odd = across(words_even, 1)
    sums.append(spread(odd, *args, [words_even]))
    sums += [over(x) for x in sums]
    pair_even_sib, _ = unpack(over(words_even))
    pair_odd, list_odd = unpack(words_odd, pair_even_sib[1:], single=True)
    pairs = [pair_even, pair_odd, pair_even_sib, unpack(over(words_odd))[0]]
    words = dict(zip(even + odd, [*list_even, *list_odd]))

    order = list(range(devices - 1, -1, -1))
    direct, hands, waits = order[:-1], {}, {}
    if devices == 8:
        order = [7, 6, 4, 5, 3, 2, 1, 0]
        direct = [7, 6, 5, 3, 2, 1]
        hands = {3: 4}
        waits = {2: [7], 1: [6]}
    halves = dict()
    pieces = dict()
    got = dict()
    out = (sums[0],) * 4
    held = (sums[0][:half, :cols],) * 2
    for k in order:
        after = list(out) + [got[x] for x in waits.get(k, [])]
        after += [out[0]] * (6 - len(after))
        if k in hands:
            held = halves[hands[k]]
        later, made, *last = out = block(words[k], sums, pairs, held, after)
        held = last
        if k in hands:
            x = hands[k]
            got[x] = across(later, x)
            pieces[x] = (got[x], got[x])
        if k in direct:
            got[k] = across(made, k)
            pieces[k] = (got[k], over(got[k][1]))
        else:
            halves[k] = (last[0], over(last[1]))
    pieces[0] = halves[0]
    return fill(order, [pieces[k] for k in order], (hit_rows, devices * cols), out[:2])


def large(fingerprints, pick_list, inverse_root):
    hit_rows, width = fingerprints.shape
    devices = lax.axis_size("hit")
    side = lax.axis_index("lm")
    half = hit_rows // 2
    weight = inverse_root[:, 0, :]
    cols = weight.shape[1]
    picks = lax.all_gather(pick_list, "lm", tiled=True)
    words = lax.all_gather(fingerprints, "hit", tiled=True)
    hits = words.shape[0]
    blocks = words.reshape(devices, hit_rows, width)

    def spread_block(index):
        hot = (index * hit_rows + jnp.arange(hit_rows))[:, None] == picks[None, :]
        made = jnp.dot(hot.astype(jnp.bfloat16), weight, preferred_element_type=jnp.float32)
        return made.astype(jnp.bfloat16)

    def flag_block(block_words):
        flags = [((block_words >> bit) & 1).astype(F8) for bit in range(BITS)]
        return jnp.concatenate(flags, axis=1)

    sums = lax.map(spread_block, jnp.arange(devices)).reshape(hits, cols)
    sums = lax.all_gather(sums, "lm", axis=1, tiled=True)
    bits = lax.map(flag_block, blocks).reshape(hits, BITS * width)
    count = jnp.sum(lax.population_count(words), axis=1).astype(jnp.float32)

    def one(index):
        start = index * hit_rows + side * half
        rows = lax.dynamic_slice_in_dim(bits, start, half)
        common = lax.dot_general(
            rows, bits, (((1,), (1,)), ((), ())), preferred_element_type=jnp.float32
        )
        union = lax.dynamic_slice_in_dim(count, start, half)[:, None] + count[None, :] - common
        kernel = (common / union).astype(jnp.bfloat16)
        return jnp.dot(kernel, sums, preferred_element_type=jnp.float32).astype(jnp.bfloat16)

    made = lax.map(one, jnp.arange(devices))
    got = lax.all_to_all(made, "hit", 0, 0, tiled=True)
    got = got.reshape(devices, half, 2, cols).transpose(2, 1, 0, 3)
    got = got.reshape(2, 1, half, devices * cols)
    return lax.all_to_all(got, "lm", 0, 1, tiled=True).reshape(hit_rows, devices * cols)


def local(fingerprints, pick_list, inverse_root):
    if lax.axis_size("hit") > 8:
        return large(fingerprints, pick_list, inverse_root)
    return small(fingerprints, pick_list, inverse_root)


def solution(mesh):
    placed = (P(("lib", "hit"), None), P(("lib", "lm")), P("lib", "lm", "hit"))
    return jax.shard_map(
        local, mesh=mesh, in_specs=placed, out_specs=P(("lib", "hit"), "lm"), check_vma=False
    )
```

```python
import functools

import jax
import jax.numpy as jnp
from jax import lax
from jax.experimental import pallas as pl
from jax.experimental.pallas import tpu as pltpu
from jax.sharding import PartitionSpec as P

F8 = jnp.float8_e4m3fn
BITS = 16
VMEM = pl.BlockSpec(memory_space=pltpu.VMEM)
ANY = pl.BlockSpec(memory_space=pl.ANY)


def unpack_kernel(*refs, count, stack, single, inputs):
    bits_ref, count_ref = refs[inputs : inputs + 2]
    more = refs[inputs + 2 :]
    word_ref = refs[0]
    if stack:
        word_ref = more[0]
        for at in range(count):
            word_ref[at] = refs[at][...]
    if single:
        for at in range(count):
            more[at - count][...] = word_ref[at]

    @pl.loop(0, count, unroll=2)
    def _(at):
        words = word_ref[at].astype(jnp.int32)
        rows, width = words.shape
        here = pl.ds(pl.multiple_of(at * rows, rows), rows)
        ones = jnp.sum(lax.population_count(words).astype(jnp.float32), axis=1, keepdims=True)
        count_ref[here, :] = jnp.broadcast_to(ones, (rows, count_ref.shape[1]))
        for bit in range(BITS):
            flag = ((words >> bit) & 1).astype(jnp.int8)
            bits_ref[here, bit * width : (bit + 1) * width] = flag.astype(F8)


def unpack(words, after=(), stack=False, single=False):
    words = list(words) if isinstance(words, (list, tuple)) else [words]
    rows, width = words[0].shape[-2:]
    count = words[0].shape[0] if len(words[0].shape) == 3 else len(words)
    shapes = [
        jax.ShapeDtypeStruct((count * rows, BITS * width), F8),
        jax.ShapeDtypeStruct((count * rows, 128), jnp.float32),
    ]
    if stack:
        shapes.append(jax.ShapeDtypeStruct((count, rows, width), words[0].dtype))
    if single:
        shapes += [jax.ShapeDtypeStruct((rows, width), words[0].dtype)] * count
    out = pl.pallas_call(
        functools.partial(
            unpack_kernel,
            count=count,
            stack=stack,
            single=single,
            inputs=len(words) + len(after),
        ),
        in_specs=[VMEM] * len(words) + [ANY] * len(after),
        out_specs=[VMEM] * len(shapes),
        out_shape=shapes,
        compiler_params=pltpu.CompilerParams(vmem_limit_bytes=24 * 2**20),
        cost_estimate=pl.CostEstimate(
            flops=4096 * count * rows * BITS * width, bytes_accessed=rows * width, transcendentals=0
        ),
        name="unpack",
    )(*words, *after)
    return tuple(out[:2]), out[2:]


def fetch_kernel(in_ref, out_ref, sem):
    copy = pltpu.make_async_copy(in_ref, out_ref, sem)
    copy.start()
    copy.wait()


def fetch(x):
    return pl.pallas_call(
        fetch_kernel,
        in_specs=[ANY],
        out_specs=VMEM,
        out_shape=jax.ShapeDtypeStruct(x.shape, x.dtype),
        scratch_shapes=[pltpu.SemaphoreType.DMA],
        compiler_params=pltpu.CompilerParams(vmem_limit_bytes=24 * 2**20),
        name="fetch",
    )(x)


def spread_kernel(mine_ref, own_ref, other_ref, sib_ref, *refs, steps, hit_rows, chunk):
    out_ref = refs[-1]
    cols = own_ref.shape[1]
    half = mine_ref.shape[1]
    rows = hit_rows // 2
    side = lax.axis_index("lm")
    me = lax.axis_index("hit")
    places = []
    for place in (side, 1 - side):
        for start in range(0, half, chunk):
            at = pl.ds(pl.multiple_of(place * half + start, chunk), chunk)
            places.append((start, at))
    parts = [
        lax.broadcasted_iota(jnp.int32, (rows, 1), 0) + ((me ^ k) * hit_rows + side * rows)
        for k in steps
    ]
    ids = jnp.concatenate(parts, axis=0)
    own = sib = None
    for i, (start, at) in enumerate(places):
        pick_ref = mine_ref if i < len(places) // 2 else other_ref
        hot = jnp.where(pick_ref[0:1, start : start + chunk] == ids, 1.0, 0.0).astype(jnp.bfloat16)
        part = jnp.dot(hot, sib_ref[at, :], preferred_element_type=jnp.float32)
        sib = part if sib is None else sib + part
        part = jnp.dot(hot, own_ref[at, :], preferred_element_type=jnp.float32)
        own = part if own is None else own + part
    out_ref[:cols, :] = own.T.astype(jnp.bfloat16)
    out_ref[cols:, :] = sib.T.astype(jnp.bfloat16)


def spread(steps, hit_rows, mine, own, other, sib, after):
    marks, cols = own.shape
    hits = len(steps) * hit_rows // 2
    chunk = 512
    return pl.pallas_call(
        functools.partial(spread_kernel, steps=steps, hit_rows=hit_rows, chunk=chunk),
        in_specs=[VMEM] * 4 + [ANY] * len(after),
        out_specs=VMEM,
        out_shape=jax.ShapeDtypeStruct((2 * cols, hits), jnp.bfloat16),
        compiler_params=pltpu.CompilerParams(vmem_limit_bytes=24 * 2**20),
        cost_estimate=pl.CostEstimate(
            flops=marks * cols * hits // 8, bytes_accessed=marks * cols, transcendentals=0
        ),
        name="spread",
    )(mine, own, other, sib, *after)


def block_kernel(words_ref, *refs, sums, pairs, tile):
    later_ref, both_ref, own_ref, sib_ref, flags, kern = refs[-6:]
    sum_refs = refs[:sums]
    pair_refs = refs[sums : sums + 2 * pairs]
    held = refs[sums + 2 * pairs : sums + 2 * pairs + 2]
    later_ref[0] = held[0][...]
    later_ref[1] = held[1][...]
    words = words_ref[...].astype(jnp.int32).T
    width = words.shape[0]
    count = jnp.sum(lax.population_count(words).astype(jnp.float32), axis=0, keepdims=True)
    for bit in range(BITS):
        flag = ((words >> bit) & 1).astype(jnp.int8)
        flags[bit * width : (bit + 1) * width, :] = flag.astype(F8)
    at = 0
    for bits_ref, count_ref in zip(pair_refs[::2], pair_refs[1::2]):
        rows = bits_ref.shape[0]
        size = min(tile, rows)
        for low in range(0, rows, size):
            here = slice(low, low + size)
            common = jnp.dot(bits_ref[here, :], flags[...], preferred_element_type=jnp.float32)
            union = (count + count_ref[here, 0:1]) - common
            kern[at : at + size, :] = (common / union).astype(jnp.bfloat16)
            at += size
    at = 0
    made = []
    for ref in sum_refs:
        rows = ref.shape[1]
        made.append(
            jnp.dot(ref[...], kern[at : at + rows, :], preferred_element_type=jnp.float32)
        )
        at += rows
    mine = sum(made[: sums // 2])
    theirs = sum(made[sums // 2 :])
    cols = mine.shape[0] // 2
    own = (mine[:cols] + theirs[cols:]).T.astype(jnp.bfloat16)
    sib = (mine[cols:] + theirs[:cols]).T.astype(jnp.bfloat16)
    both_ref[0] = own
    both_ref[1] = sib
    own_ref[...] = own
    sib_ref[...] = sib


def block(words, sums, pairs, held, after):
    rows, width = words.shape
    cols = sums[0].shape[0] // 2
    hits = sum(x.shape[1] for x in sums)
    flat = [x for pair in pairs for x in pair] + list(held)
    one = jax.ShapeDtypeStruct((rows, cols), jnp.bfloat16)
    both = jax.ShapeDtypeStruct((2, rows, cols), jnp.bfloat16)
    return pl.pallas_call(
        functools.partial(block_kernel, sums=len(sums), pairs=len(pairs), tile=512),
        in_specs=[VMEM] * (1 + len(sums) + len(flat)) + [ANY] * len(after),
        out_specs=[VMEM] * 4,
        out_shape=[both, both, one, one],
        scratch_shapes=[
            pltpu.VMEM((BITS * width, rows), F8),
            pltpu.VMEM((hits, rows), jnp.bfloat16),
        ],
        compiler_params=pltpu.CompilerParams(vmem_limit_bytes=32 * 2**20),
        cost_estimate=pl.CostEstimate(
            flops=2 * hits * rows * (BITS * width + 2 * cols),
            bytes_accessed=rows * cols,
            transcendentals=0,
        ),
        name="block",
    )(words, *sums, *flat, *after)


def fill_kernel(*refs, steps):
    out_ref = refs[-1]
    side = lax.axis_index("lm")
    me = lax.axis_index("hit")
    rows, cols = refs[1].shape[-2:]
    band = rows // 4

    @pl.loop(0, rows // band)
    def _(step):
        low = pl.multiple_of(step * band, band)
        for i, k in enumerate(steps):
            for at, which in ((0, side), (1, 1 - side)):
                ref = refs[2 * i + at]
                here = pl.ds(low, band)
                piece = ref[at, here, :] if len(ref.shape) == 3 else ref[here, :]
                row = pl.ds(pl.multiple_of(which * rows + low, band), band)
                out_ref[row, pl.ds(pl.multiple_of((me ^ k) * cols, cols), cols)] = piece


def fill(steps, pieces, shape, after):
    return pl.pallas_call(
        functools.partial(fill_kernel, steps=steps),
        in_specs=[VMEM] * (2 * len(pieces)) + [ANY] * len(after),
        out_specs=VMEM,
        out_shape=jax.ShapeDtypeStruct(shape, jnp.bfloat16),
        compiler_params=pltpu.CompilerParams(vmem_limit_bytes=16 * 2**20),
        name="fill",
    )(*[x for piece in pieces for x in piece], *after)


def small(fingerprints, pick_list, inverse_root):
    hit_rows, width = fingerprints.shape
    devices = lax.axis_size("hit")
    side = lax.axis_index("lm")
    half = hit_rows // 2
    weight = inverse_root[:, 0, :]
    cols = weight.shape[1]

    def across(x, k):
        return lax.ppermute(x, "hit", [(i, i ^ k) for i in range(devices)])

    def over(x):
        return lax.ppermute(x, "lm", [(0, 1), (1, 0)])

    mine = lax.dynamic_slice_in_dim(fingerprints, side * half, half).astype(jnp.uint16)
    other_picks = over(pick_list)
    other_weight = over(weight)

    even = list(range(0, devices, 2))
    odd = [k ^ 1 for k in even]
    words_z = [across(mine, k) if k else mine for k in even]

    args = (hit_rows, pick_list.reshape(1, -1), fetch(weight), other_picks.reshape(1, -1), other_weight)
    sums = [spread(even, *args, [])]
    pair_even, (words_even, *list_even) = unpack(words_z, sums, True, True)
    words_odd = across(words_even, 1)
    sums.append(spread(odd, *args, [words_even]))
    sums += [over(x) for x in sums]
    pair_even_sib, _ = unpack(over(words_even))
    pair_odd, list_odd = unpack(words_odd, pair_even_sib[1:], single=True)
    pairs = [pair_even, pair_odd, pair_even_sib, unpack(over(words_odd))[0]]
    words = dict(zip(even + odd, [*list_even, *list_odd]))

    order = list(range(devices - 1, -1, -1))
    direct, hands, waits = order[:-1], {}, {}
    if devices == 8:
        order = [7, 6, 4, 5, 3, 2, 1, 0]
        direct = [7, 6, 5, 3, 2, 1]
        hands = {3: 4}
        waits = {2: [7], 1: [6]}
    halves = dict()
    pieces = dict()
    got = dict()
    out = (sums[0],) * 4
    held = (sums[0][:half, :cols],) * 2
    for k in order:
        after = list(out) + [got[x] for x in waits.get(k, [])]
        after += [out[0]] * (6 - len(after))
        if k in hands:
            held = halves[hands[k]]
        later, made, *last = out = block(words[k], sums, pairs, held, after)
        held = last
        if k in hands:
            x = hands[k]
            got[x] = across(later, x)
            pieces[x] = (got[x], got[x])
        if k in direct:
            got[k] = across(made, k)
            pieces[k] = (got[k], over(got[k][1]))
        else:
            halves[k] = (last[0], over(last[1]))
    pieces[0] = halves[0]
    return fill(order, [pieces[k] for k in order], (hit_rows, devices * cols), out[:2])


def large(fingerprints, pick_list, inverse_root):
    hit_rows, width = fingerprints.shape
    devices = lax.axis_size("hit")
    side = lax.axis_index("lm")
    half = hit_rows // 2
    weight = inverse_root[:, 0, :]
    cols = weight.shape[1]
    picks = lax.all_gather(pick_list, "lm", tiled=True)
    words = lax.all_gather(fingerprints, "hit", tiled=True)
    hits = words.shape[0]
    blocks = words.reshape(devices, hit_rows, width)

    def spread_block(index):
        hot = (index * hit_rows + jnp.arange(hit_rows))[:, None] == picks[None, :]
        made = jnp.dot(hot.astype(jnp.bfloat16), weight, preferred_element_type=jnp.float32)
        return made.astype(jnp.bfloat16)

    def flag_block(block_words):
        flags = [((block_words >> bit) & 1).astype(F8) for bit in range(BITS)]
        return jnp.concatenate(flags, axis=1)

    sums = lax.map(spread_block, jnp.arange(devices)).reshape(hits, cols)
    sums = lax.all_gather(sums, "lm", axis=1, tiled=True)
    bits = lax.map(flag_block, blocks).reshape(hits, BITS * width)
    count = jnp.sum(lax.population_count(words), axis=1).astype(jnp.float32)

    def one(index):
        start = index * hit_rows + side * half
        rows = lax.dynamic_slice_in_dim(bits, start, half)
        common = lax.dot_general(
            rows, bits, (((1,), (1,)), ((), ())), preferred_element_type=jnp.float32
        )
        union = lax.dynamic_slice_in_dim(count, start, half)[:, None] + count[None, :] - common
        kernel = (common / union).astype(jnp.bfloat16)
        return jnp.dot(kernel, sums, preferred_element_type=jnp.float32).astype(jnp.bfloat16)

    made = lax.map(one, jnp.arange(devices))
    got = lax.all_to_all(made, "hit", 0, 0, tiled=True)
    got = got.reshape(devices, half, 2, cols).transpose(2, 1, 0, 3)
    got = got.reshape(2, 1, half, devices * cols)
    return lax.all_to_all(got, "lm", 0, 1, tiled=True).reshape(hit_rows, devices * cols)


def local(fingerprints, pick_list, inverse_root):
    if lax.axis_size("hit") > 8:
        return large(fingerprints, pick_list, inverse_root)
    return small(fingerprints, pick_list, inverse_root)


def solution(mesh):
    placed = (P(("lib", "hit"), None), P(("lib", "lm")), P("lib", "lm", "hit"))
    return jax.shard_map(
        local, mesh=mesh, in_specs=placed, out_specs=P(("lib", "hit"), "lm"), check_vma=False
    )
```
